32 devices in a mesh: dp: 8 (over z, y), expert: 4 (over x, core).
Axes of the slice: x: 2, y: 2, z: 4, core: 2. Of those that a mesh axis runs over, the one named last changes fastest.
Arguments:
- residual: bfloat16 [512, 4096], P(('dp', 'expert')), may hold values from -8.2 to 8.2
- queries: bfloat16 [512, 4096], P('dp', 'expert'), may hold values from -24 to 24
- new_keys: bfloat16 [512, 1024], P('dp', 'expert'), may hold values from -6 to 6
- new_values: bfloat16 [512, 1024], P('dp', 'expert'), may hold values from -6 to 6
- cache_keys: bfloat16 [16, 1024, 1024], P('dp', None, 'expert'), may hold values from -8 to 8
- cache_values: bfloat16 [16, 1024, 1024], P('dp', None, 'expert'), may hold values from -6 to 6
- out_weight: bfloat16 [4096, 4096], P('expert', 'dp'), may hold values from -1 to 1
- ffn_gain: float32 [4096], replicated, may hold values from 0.1 to 1.9
- router: bfloat16 [4096, 8], replicated, may hold values from -0.0234375 to 0.0234375
- routes: int32 [512, 2], P(('dp', 'expert')), may hold values from 0 to 7, all different within a row; in each aligned block of 64 rows (0 to 63, 64 to 127, ...) at most 24 rows name the same one
- w_gate: bfloat16 [8, 4096, 14336], P('expert', None, 'dp'), may hold values from -0.09375 to 0.09375
- w_up: bfloat16 [8, 4096, 14336], P('expert', None, 'dp'), may hold values from -0.09375 to 0.09375
- w_down: bfloat16 [8, 14336, 4096], P('expert', 'dp'), may hold values from -0.046875 to 0.046875
- summary_gain: float32 [4096], P('expert'), may hold values from 0.1 to 1.9
- reduce_scale: float32 [32], P('expert'), may hold values from 0.1 to 30
- assign: int32 [16], replicated, may hold values from 0 to 3
Outputs:
- summary: bfloat16 [16, 4096], P('dp', 'expert')
- reduced: bfloat16 [16, 4096], P('dp', 'expert')
The draws below stay inside these ranges and needn't reach their ends.
Inputs may be any that keep to these rules, and one draw needn't show every extreme that they name: `routes`: each token names 2 different experts and every expert is named by some token; among the tokens of one dp index (aligned blocks of 64 rows) no expert is named by more than 24 tokens, and that bound is reached in some block.
All inputs are finite; a program needn't handle non-finite values.
Results may differ from the reference program's by a relative error of at most 0.017.
Values may be sent and summed in bfloat16 or wider, within the bound.
A program may use at most 192 MiB of HBM per device.

```python
import math
import jax
import jax.numpy as jnp
import numpy as np
from jax import lax

D = 4096
HEADS = 32
KVH = 8
HD = 128
EXPERTS = 8
FF = 14336
TOPK = 2
WIN = 32
CACHE = 1024
SPAN_DEV = 2
REDUCERS = 4
SPANS = 16
TOKENS = 512
GROUP_CAP = 24
N_DP = 8


def drawn(key):
    key_query, key_cache = jax.random.split(jax.random.fold_in(key, 29), 2)
    query = jnp.clip(jax.random.normal(key_query, (TOKENS, HEADS * HD), jnp.float32), -6.0, 6.0)
    cache = jnp.clip(jax.random.normal(key_cache, (SPANS, CACHE, KVH * HD), jnp.float32), -6.0, 6.0)
    return (query, cache)


def draw_queries(key, part):
    return drawn(key)[0].astype(jnp.bfloat16)


def draw_cache_keys(key, part):
    return drawn(key)[1].astype(jnp.bfloat16)


def draw_residual(key, part):
    key_base, key_cols = jax.random.split(jax.random.fold_in(key, 11), 2)
    ramp = 0.5 + jnp.arange(D, dtype=jnp.float32) / D
    column = ramp * jnp.exp(jax.random.uniform(key_cols, (D,), jnp.float32, math.log(0.6), math.log(1.6)))
    values = 0.5 * jnp.clip(jax.random.normal(key_base, (TOKENS, D), jnp.float32), -6.0, 6.0) * column
    return values.astype(jnp.bfloat16)


def draw_reduce_scale(key, part):
    low_end = math.log(0.1)
    high_end = math.log(0.3)
    return jnp.exp(jax.random.uniform(jax.random.fold_in(key, 43), (HEADS,), jnp.float32, low_end, high_end))


def with_ends(result, rng, least, top_value):
    spot = [jax.random.randint(jax.random.fold_in(rng, axis), (), 0, length) for axis, length in enumerate(result.shape)]
    main_axis = result.shape.index(max(result.shape))
    neighbour = spot[:main_axis] + [(spot[main_axis] + 1) % result.shape[main_axis]] + spot[main_axis + 1:]
    return result.at[tuple(spot)].set(least).at[tuple(neighbour)].set(top_value)


def shard_levels(stream_key, extent, cuts, smallest, largest):
    def one(position, parts):
        steps = jax.random.uniform(jax.random.fold_in(jax.random.fold_in(stream_key, 6), position), (parts,), jnp.float32, smallest / len(cuts), largest / len(cuts))
        return jnp.repeat(jnp.exp(steps), extent[position] // parts).reshape((-1,) + (1,) * (len(extent) - position - 1))

    factor_of = one(*cuts[0])
    for cut in cuts[1:]:
        factor_of = factor_of * one(*cut)
    return factor_of


def deal_out(own_key, own, number, rows, amount, top, reach, slope):
    order = jax.random.permutation(own_key, amount)
    heavy_load, common = load_shares(amount, rows * top, reach, slope, True), load_shares(amount, rows * top, reach, slope, False)
    places = jnp.arange(amount)

    def named(lengths, turn):
        used = int((lengths > 0).sum())
        fixed = max(1, used // 4)
        passed = fixed + (places - fixed + turn * (used - fixed)) % max(1, amount - fixed)
        return jnp.zeros((amount,), jnp.int32).at[order[jnp.where(places < fixed, places, passed)]].set(jnp.asarray(lengths, jnp.int32))

    lengths = jnp.where(number % 4 == 0, named(heavy_load, number // 4), named(common, number - number // 4 - 1))
    mixed = jax.random.permutation(jax.random.fold_in(own, 3), amount)
    giver, receiver = mixed[0:amount // 2 * 2:2], mixed[1:amount // 2 * 2:2]
    room = jnp.minimum(lengths[giver] - 1, reach - lengths[receiver]) // 2
    room = jnp.where((giver == order[0]) | (receiver == order[0]) | (lengths[receiver] == 0), 0, jnp.maximum(room, 0))
    passed = jax.random.randint(jax.random.fold_in(own, 4), (amount // 2,), 0, 1 << 20) % (room + 1)
    lengths = lengths.at[giver].add(-passed).at[receiver].add(passed)
    labels = jnp.searchsorted(jnp.cumsum(lengths), jnp.arange(rows * top), side="right").astype(jnp.int32)
    grid = labels.reshape(top, rows).T
    grid = grid[jax.random.permutation(jax.random.fold_in(own, 1), rows)]
    turn = jax.random.randint(jax.random.fold_in(own, 2), (rows, 1), 0, top)
    return jnp.take_along_axis(grid, (jnp.arange(top)[None, :] + turn) % top, axis=1)


def load_shares(amount, total, most, skew, full):
    portions = [(1 << 20) // math.isqrt(standing ** skew) + 1 for standing in range(1, amount + 1)]
    largest = most if full else min(most, max(-(-total // amount), total * portions[0] // sum(portions)))
    least = 1 if total - largest >= amount - 1 else 0
    given, surplus = [largest] + [least] * (amount - 1), total - largest - least * (amount - 1)
    while surplus > 0:
        candidates = [i for i in range(1, amount) if given[i] < largest] or [i for i in range(1, amount) if given[i] < most]
        whole, remaining = sum([portions[i] for i in candidates]), surplus
        for i in candidates:
            addition = min(most - given[i], max(1, remaining * portions[i] // whole), surplus)
            given[i] = given[i] + addition
            surplus = surplus - addition
    return np.array(given)


def gaussian(key, shape, scale, bound, cuts=(), kind=jnp.bfloat16):
    loudness = shard_levels(key, shape, cuts, -0.22, 0.18) if cuts else 1.0
    result = jax.random.normal(key, shape, jnp.float32) * scale * loudness
    return jnp.minimum(jnp.maximum(result, -bound), bound).astype(kind)


def setup_inputs(seed: int = 0) -> dict:
    seeds = jax.random.split(jax.random.key(seed), 17)
    residual = draw_residual(jax.random.fold_in(seeds[16], 71), 0)
    queries = draw_queries(jax.random.fold_in(seeds[16], 71), 0)
    new_keys = gaussian(seeds[2], (TOKENS, KVH * HD), 1.0, 6.0, ((0, 8), (1, 4)))
    new_values = gaussian(seeds[3], (TOKENS, KVH * HD), 1.0, 6.0, ((0, 8), (1, 4)))
    cache_keys = draw_cache_keys(jax.random.fold_in(seeds[16], 71), 0)
    cache_values = gaussian(seeds[5], (SPANS, CACHE, KVH * HD), 1.0, 6.0, ((0, 8), (2, 4)))
    out_weight = gaussian(seeds[6], (HEADS * HD, D), HEADS ** -0.5, 1.0, ((0, 4), (1, 8)))
    ffn_gain = jnp.clip(1.0 + 0.18 * jax.random.normal(seeds[7], (D,), jnp.float32), 0.1, 1.9)
    router = gaussian(seeds[8], (D, EXPERTS), (16 * D) ** -0.5, 0.0234375)
    routes_keys = jax.random.split(jax.random.fold_in(seeds[9], 1), TOKENS // (SPAN_DEV * WIN))
    routes_turns = jax.random.permutation(jax.random.fold_in(seeds[9], 3), TOKENS // (SPAN_DEV * WIN))
    routes = jax.vmap(lambda own, number: deal_out(jax.random.fold_in(seeds[9], 2), own, number, SPAN_DEV * WIN, EXPERTS, TOPK, GROUP_CAP, 2))(routes_keys, routes_turns).reshape((TOKENS, TOPK))
    w_gate = gaussian(seeds[10], (EXPERTS, D, FF), D ** -0.5, 0.09375, ((0, 4), (2, 8)))
    w_up = gaussian(seeds[11], (EXPERTS, D, FF), D ** -0.5, 0.09375, ((0, 4), (2, 8)))
    w_down = gaussian(seeds[12], (EXPERTS, FF, D), FF ** -0.5, 0.046875, ((0, 4), (1, 8)))
    summary_gain = jnp.clip(1.0 + 0.18 * jax.random.normal(seeds[13], (D,), jnp.float32), 0.1, 1.9)
    reduce_scale = draw_reduce_scale(jax.random.fold_in(seeds[16], 71), 0)
    assign = with_ends(jax.random.randint(seeds[15], (SPANS,), 0, REDUCERS), jax.random.fold_in(seeds[15], 1), 0, REDUCERS - 1).astype(jnp.int32)
    return {"residual": residual, "queries": queries, "new_keys": new_keys, "new_values": new_values, "cache_keys": cache_keys, "cache_values": cache_values, "out_weight": out_weight, "ffn_gain": ffn_gain, "router": router, "routes": routes, "w_gate": w_gate, "w_up": w_up, "w_down": w_down, "summary_gain": summary_gain, "reduce_scale": reduce_scale, "assign": assign}


EPSILON = 1e-05

def attend(queries, new_keys, new_values, cache_keys, cache_values):
    span_count, cache_len, kv_width = cache_keys.shape
    kv_local = kv_width // HD
    group = HEADS // KVH
    window = queries.shape[0] // span_count
    query_view = queries.reshape(span_count, window, kv_local, group, HD).astype(jnp.float32)
    fresh_keys = new_keys.reshape(span_count, window, kv_local, HD).astype(jnp.float32)
    fresh_values = new_values.reshape(span_count, window, kv_local, HD).astype(jnp.float32)
    stored_keys = cache_keys.reshape(span_count, cache_len, kv_local, HD).astype(jnp.float32)
    stored_values = cache_values.reshape(span_count, cache_len, kv_local, HD).astype(jnp.float32)
    factor = 1.0 / math.sqrt(HD)
    past_scores = jnp.einsum('ctkgd,cpkd->ckgtp', query_view, stored_keys) * factor
    fresh_scores = jnp.einsum('ctkgd,cskd->ckgts', query_view, fresh_keys) * factor
    causal = jnp.arange(window)[:, None] >= jnp.arange(window)[None, :]
    fresh_scores = jnp.where(causal, fresh_scores, -jnp.inf)
    highest = jnp.maximum(lax.optimization_barrier(jnp.max(past_scores, axis=-1)), lax.optimization_barrier(jnp.max(fresh_scores, axis=-1)))[..., None]
    past_exp = jnp.exp(past_scores - highest)
    fresh_exp = jnp.exp(fresh_scores - highest)
    totals = lax.optimization_barrier(jnp.sum(past_exp, axis=-1, keepdims=True)) + lax.optimization_barrier(jnp.sum(fresh_exp, axis=-1, keepdims=True))
    past_weights = (past_exp / totals).astype(jnp.bfloat16).astype(jnp.float32)
    fresh_weights = (fresh_exp / totals).astype(jnp.bfloat16).astype(jnp.float32)
    context = jnp.einsum('ckgtp,cpkd->ctkgd', past_weights, stored_values)
    context = context + jnp.einsum('ckgts,cskd->ctkgd', fresh_weights, fresh_values)
    return context.astype(jnp.bfloat16).reshape(span_count * window, kv_local * group * HD)

def reference(residual, queries, new_keys, new_values, cache_keys, cache_values, out_weight, ffn_gain, router, routes, w_gate, w_up, w_down, summary_gain, reduce_scale, assign):
    per_span = (queries.reshape(SPANS, WIN, HEADS * HD), new_keys.reshape(SPANS, WIN, KVH * HD), new_values.reshape(SPANS, WIN, KVH * HD), cache_keys, cache_values)

    def one_span(items):
        return attend(items[0], items[1], items[2], items[3][None], items[4][None])
    attended = lax.map(one_span, per_span).reshape(TOKENS, HEADS * HD)
    mixed = residual.astype(jnp.float32) + jnp.dot(attended, out_weight, preferred_element_type=jnp.float32)
    normed = (mixed * lax.rsqrt(lax.optimization_barrier(jnp.mean(mixed * mixed, axis=-1, keepdims=True)) + EPSILON) * ffn_gain).astype(jnp.bfloat16)
    logits = jnp.dot(normed, router, preferred_element_type=jnp.float32)
    expert_ids = jnp.arange(EXPERTS, dtype=jnp.int32)
    first = routes[:, 0:1] == expert_ids[None, :]
    second = routes[:, 1:2] == expert_ids[None, :]
    first_logit = lax.optimization_barrier(jnp.sum(jnp.where(first, logits, 0.0), axis=-1))
    second_logit = lax.optimization_barrier(jnp.sum(jnp.where(second, logits, 0.0), axis=-1))
    gates = jnp.stack([jax.nn.sigmoid(first_logit - second_logit), jax.nn.sigmoid(second_logit - first_logit)], axis=1)
    slot_total = N_DP * GROUP_CAP

    def expert_pass(running, expert):
        chosen = routes == expert
        gate_here = lax.optimization_barrier(jnp.sum(jnp.where(chosen, gates, 0.0), axis=1))
        member = jnp.any(chosen, axis=1)
        place = jnp.cumsum(member.astype(jnp.int32)) - 1
        target = jnp.where(member, place, slot_total).astype(jnp.int32)
        index = jnp.zeros((slot_total,), jnp.int32).at[target].set(jnp.arange(TOKENS, dtype=jnp.int32), mode='drop')
        filled = jnp.arange(slot_total, dtype=jnp.int32) < jnp.sum(member.astype(jnp.int32))
        rows = normed[index]
        gate_matrix = lax.dynamic_index_in_dim(w_gate, expert, 0, keepdims=False)
        up_matrix = lax.dynamic_index_in_dim(w_up, expert, 0, keepdims=False)
        down_matrix = lax.dynamic_index_in_dim(w_down, expert, 0, keepdims=False)
        gate_proj = jnp.dot(rows, gate_matrix, preferred_element_type=jnp.float32)
        up_proj = jnp.dot(rows, up_matrix, preferred_element_type=jnp.float32)
        hidden = (jax.nn.silu(gate_proj) * up_proj).astype(jnp.bfloat16)
        outputs = jnp.dot(hidden, down_matrix, preferred_element_type=jnp.float32)
        weight = jnp.where(filled, gate_here[index], 0.0)
        return (running.at[index].add(weight[:, None] * outputs), None)
    moe, unused = lax.scan(expert_pass, jnp.zeros((TOKENS, D), jnp.float32), expert_ids)
    token_out = mixed + moe
    pooled = lax.optimization_barrier(jnp.sum(token_out.reshape(SPANS, WIN, D), axis=1))
    summary = (pooled * lax.rsqrt(lax.optimization_barrier(jnp.mean(pooled * pooled, axis=-1, keepdims=True)) + EPSILON) * summary_gain).astype(jnp.bfloat16)
    heads = summary.reshape(SPANS, HEADS, HD).astype(jnp.float32)
    factor = reduce_scale / math.sqrt(HD)
    scores = jnp.einsum('chd,khd->hck', heads, heads) * factor[:, None, None]
    same = assign[:, None] == assign[None, :]
    scores = jnp.where(same[None], scores, -jnp.inf)
    highest = lax.optimization_barrier(jnp.max(scores, axis=-1, keepdims=True))
    expo = jnp.exp(scores - highest)
    weights = (expo / lax.optimization_barrier(jnp.sum(expo, axis=-1, keepdims=True))).astype(jnp.bfloat16).astype(jnp.float32)
    reduced = jnp.einsum('hck,khd->chd', weights, heads).reshape(SPANS, D).astype(jnp.bfloat16)
    return (summary, reduced)
```

```python
import math

import jax
import jax.numpy as jnp
from jax import lax
from jax.sharding import PartitionSpec as P

HEADS = 32
KVH = 8
HD = 128
EXPERTS = 8
WIN = 32
GROUP_CAP = 24


EPSILON = 1e-05


def attend(queries, new_keys, new_values, cache_keys, cache_values):
    span_count, cache_len, kv_width = cache_keys.shape
    kv_local = kv_width // HD
    group = HEADS // KVH
    window = queries.shape[0] // span_count
    query_view = queries.reshape(span_count, window, kv_local, group, HD)
    fresh_keys = new_keys.reshape(span_count, window, kv_local, HD)
    fresh_values = new_values.reshape(span_count, window, kv_local, HD)
    stored_keys = cache_keys.reshape(span_count, cache_len, kv_local, HD)
    stored_values = cache_values.reshape(span_count, cache_len, kv_local, HD)
    factor = 1.0 / math.sqrt(HD)
    past_scores = (
        jnp.einsum("ctkgd,cpkd->ckgtp", query_view, stored_keys, preferred_element_type=jnp.float32)
        * factor
    )
    fresh_scores = (
        jnp.einsum("ctkgd,cskd->ckgts", query_view, fresh_keys, preferred_element_type=jnp.float32)
        * factor
    )
    causal = jnp.arange(window)[:, None] >= jnp.arange(window)[None, :]
    fresh_scores = jnp.where(causal, fresh_scores, -jnp.inf)
    highest = jnp.maximum(jnp.max(past_scores, axis=-1), jnp.max(fresh_scores, axis=-1))[..., None]
    past_exp = jnp.exp(past_scores - highest)
    fresh_exp = jnp.exp(fresh_scores - highest)
    totals = jnp.sum(past_exp, axis=-1, keepdims=True) + jnp.sum(fresh_exp, axis=-1, keepdims=True)
    past_weights = (past_exp / totals).astype(jnp.bfloat16)
    fresh_weights = (fresh_exp / totals).astype(jnp.bfloat16)
    context = jnp.einsum(
        "ckgtp,cpkd->ctkgd", past_weights, stored_values, preferred_element_type=jnp.float32
    )
    context = context + jnp.einsum(
        "ckgts,cskd->ctkgd", fresh_weights, fresh_values, preferred_element_type=jnp.float32
    )
    return context.astype(jnp.bfloat16).reshape(span_count * window, kv_local * group * HD)


def expert_rows(rows, w_gate, w_up, w_down):
    gate_proj = jnp.einsum("ned,edf->nef", rows, w_gate, preferred_element_type=jnp.float32)
    up_proj = jnp.einsum("ned,edf->nef", rows, w_up, preferred_element_type=jnp.float32)
    hidden = (jax.nn.silu(gate_proj) * up_proj).astype(jnp.bfloat16)
    return jnp.einsum("nef,efd->ned", hidden, w_down, preferred_element_type=jnp.float32)


def shards(
    residual,
    queries,
    new_keys,
    new_values,
    cache_keys,
    cache_values,
    out_weight,
    ffn_gain,
    router,
    routes,
    w_gate,
    w_up,
    w_down,
    summary_gain,
    reduce_scale,
    assign,
):
    expert_count = lax.axis_size("expert")
    dp_index = lax.axis_index("dp")
    column = lax.axis_index("expert")
    span_local = cache_keys.shape[0]
    tok_local = residual.shape[0]
    width = residual.shape[1]
    slice_width = width // expert_count
    highest_precision = lax.Precision.HIGHEST
    attended = attend(queries, new_keys, new_values, cache_keys, cache_values)
    head_terms = jnp.dot(
        attended,
        lax.all_gather(out_weight, "dp", axis=1, tiled=True),
        preferred_element_type=jnp.float32,
    )
    mixed = residual.astype(jnp.float32) + lax.psum_scatter(
        head_terms, "expert", scatter_dimension=0, tiled=True
    )
    normed = (
        mixed * lax.rsqrt(jnp.mean(mixed * mixed, axis=-1, keepdims=True) + EPSILON) * ffn_gain
    ).astype(jnp.bfloat16)
    logits = jnp.dot(normed, router, preferred_element_type=jnp.float32)
    expert_ids = jnp.arange(EXPERTS, dtype=jnp.int32)
    first = routes[:, 0:1] == expert_ids[None, :]
    second = routes[:, 1:2] == expert_ids[None, :]
    first_logit = jnp.sum(jnp.where(first, logits, 0.0), axis=-1)
    second_logit = jnp.sum(jnp.where(second, logits, 0.0), axis=-1)
    partner = jnp.where(first, routes[:, 1:2], jnp.where(second, routes[:, 0:1], -1))
    outgoing = jnp.where((partner >= 0).T[:, :, None], normed[None, :, :], 0)
    arrived_rows, arrived_partner = (
        lax.all_to_all(outgoing, "expert", split_axis=0, concat_axis=1, tiled=True),
        lax.all_to_all(partner.T, "expert", split_axis=0, concat_axis=1, tiled=True),
    )
    present = (arrived_partner >= 0).astype(jnp.int32)
    slots = jnp.arange(present.shape[1])
    earlier = slots[:, None] < slots[None, :]
    position = jnp.sum(jnp.where(earlier[None], present[:, :, None], 0), axis=1)
    picker = (present[:, None, :] > 0) & (
        position[:, None, :] == jnp.arange(GROUP_CAP)[None, :, None]
    )
    compact = jnp.einsum(
        "eks,esd->ked",
        picker.astype(jnp.bfloat16),
        arrived_rows,
        preferred_element_type=jnp.float32,
    ).astype(jnp.bfloat16)
    token_span = (column * tok_local + jnp.arange(tok_local)) // WIN
    pool_matrix = (token_span[None, :] == jnp.arange(span_local)[:, None]).astype(jnp.float32)
    gathered = lax.all_gather(compact, "dp", axis=0, tiled=True)
    returned = lax.psum_scatter(
        expert_rows(gathered, w_gate, w_up, w_down), "dp", scatter_dimension=0, tiled=True
    )
    spread = jnp.einsum(
        "eks,ked->esd", picker.astype(jnp.float32), returned, precision=highest_precision
    )
    back = lax.all_to_all(spread, "expert", split_axis=1, concat_axis=0, tiled=True)
    gate_table = jnp.where(first, jax.nn.sigmoid(first_logit - second_logit)[:, None], 0.0)
    gate_table = gate_table + jnp.where(
        second, jax.nn.sigmoid(second_logit - first_logit)[:, None], 0.0
    )
    token_out = mixed + jnp.einsum("te,etd->td", gate_table, back, precision=highest_precision)
    pooled_local = jnp.dot(pool_matrix, token_out, precision=highest_precision)
    pooled = lax.psum_scatter(pooled_local, "expert", scatter_dimension=1, tiled=True)
    squares = lax.psum(jnp.sum(pooled * pooled, axis=-1), "expert")
    summary = (pooled * lax.rsqrt(squares / width + EPSILON)[:, None] * summary_gain).astype(
        jnp.bfloat16
    )
    everyone = lax.all_gather(summary, "dp", axis=0, tiled=True)
    heads_local = slice_width // HD
    mine = summary.reshape(span_local, heads_local, HD)
    others = everyone.reshape(everyone.shape[0], heads_local, HD)
    factor = reduce_scale / math.sqrt(HD)
    scores = (
        jnp.einsum("chd,khd->hck", mine, others, preferred_element_type=jnp.float32)
        * factor[:, None, None]
    )
    own_assign = lax.dynamic_slice_in_dim(assign, dp_index * span_local, span_local)
    same = own_assign[:, None] == assign[None, :]
    scores = jnp.where(same[None], scores, -jnp.inf)
    highest = jnp.max(scores, axis=-1, keepdims=True)
    expo = jnp.exp(scores - highest)
    weights = (expo / jnp.sum(expo, axis=-1, keepdims=True)).astype(jnp.bfloat16)
    reduced = jnp.einsum("hck,khd->chd", weights, others, preferred_element_type=jnp.float32)
    reduced = reduced.reshape(span_local, slice_width).astype(jnp.bfloat16)
    return (summary, reduced)


def solution(mesh):
    return jax.shard_map(
        shards,
        mesh=mesh,
        in_specs=(
            P(("dp", "expert"), None),
            P("dp", "expert"),
            P("dp", "expert"),
            P("dp", "expert"),
            P("dp", None, "expert"),
            P("dp", None, "expert"),
            P("expert", "dp"),
            P(),
            P(),
            P(("dp", "expert"), None),
            P("expert", None, "dp"),
            P("expert", None, "dp"),
            P("expert", "dp", None),
            P("expert"),
            P("expert"),
            P(),
        ),
        out_specs=(P("dp", "expert"), P("dp", "expert")),
        check_vma=False,
    )
```

```python
import math

import jax
import jax.numpy as jnp
from jax import lax
from jax.sharding import PartitionSpec as P

HEADS = 32
KVH = 8
HD = 128
EXPERTS = 8
WIN = 32
GROUP_CAP = 24


EPSILON = 1e-05


def attend(queries, new_keys, new_values, cache_keys, cache_values):
    span_count, cache_len, kv_width = cache_keys.shape
    kv_local = kv_width // HD
    group = HEADS // KVH
    window = queries.shape[0] // span_count
    query_view = queries.reshape(span_count, window, kv_local, group, HD)
    fresh_keys = new_keys.reshape(span_count, window, kv_local, HD)
    fresh_values = new_values.reshape(span_count, window, kv_local, HD)
    stored_keys = cache_keys.reshape(span_count, cache_len, kv_local, HD)
    stored_values = cache_values.reshape(span_count, cache_len, kv_local, HD)
    factor = 1.0 / math.sqrt(HD)
    past_scores = (
        jnp.einsum("ctkgd,cpkd->ckgtp", query_view, stored_keys, preferred_element_type=jnp.float32)
        * factor
    )
    fresh_scores = (
        jnp.einsum("ctkgd,cskd->ckgts", query_view, fresh_keys, preferred_element_type=jnp.float32)
        * factor
    )
    causal = jnp.arange(window)[:, None] >= jnp.arange(window)[None, :]
    fresh_scores = jnp.where(causal, fresh_scores, -jnp.inf)
    highest = jnp.maximum(jnp.max(past_scores, axis=-1), jnp.max(fresh_scores, axis=-1))[..., None]
    past_exp = jnp.exp(past_scores - highest)
    fresh_exp = jnp.exp(fresh_scores - highest)
    totals = jnp.sum(past_exp, axis=-1, keepdims=True) + jnp.sum(fresh_exp, axis=-1, keepdims=True)
    past_weights = (past_exp / totals).astype(jnp.bfloat16)
    fresh_weights = (fresh_exp / totals).astype(jnp.bfloat16)
    context = jnp.einsum(
        "ckgtp,cpkd->ctkgd", past_weights, stored_values, preferred_element_type=jnp.float32
    )
    context = context + jnp.einsum(
        "ckgts,cskd->ctkgd", fresh_weights, fresh_values, preferred_element_type=jnp.float32
    )
    return context.astype(jnp.bfloat16).reshape(span_count * window, kv_local * group * HD)


def shards(
    residual,
    queries,
    new_keys,
    new_values,
    cache_keys,
    cache_values,
    out_weight,
    ffn_gain,
    router,
    routes,
    w_gate,
    w_up,
    w_down,
    summary_gain,
    reduce_scale,
    assign,
):
    n_dp, n_ex = lax.axis_size("dp"), lax.axis_size("expert")
    dp_index, column = lax.axis_index("dp"), lax.axis_index("expert")
    both = ("dp", "expert")
    span_local = cache_keys.shape[0]
    tok_local, width = residual.shape
    tokens = tok_local * n_dp * n_ex
    spans = span_local * n_dp
    exact = lax.Precision.HIGHEST
    all_routes = lax.all_gather(routes, both, axis=0, tiled=True)
    attended = attend(queries, new_keys, new_values, cache_keys, cache_values)
    rows = lax.all_gather(attended, "dp", axis=0, tiled=True)
    parts = jnp.dot(rows, out_weight, preferred_element_type=jnp.float32).astype(jnp.bfloat16)
    parts = lax.all_to_all(
        parts.reshape(n_dp * n_ex, tok_local, -1), both, split_axis=0, concat_axis=0, tiled=True
    )
    terms = jnp.sum(parts.reshape(n_dp, n_ex, tok_local, -1).astype(jnp.float32), axis=1)
    mixed = residual.astype(jnp.float32) + terms.transpose(1, 0, 2).reshape(tok_local, width)
    normed = (
        mixed * lax.rsqrt(jnp.mean(mixed * mixed, axis=-1, keepdims=True) + EPSILON) * ffn_gain
    ).astype(jnp.bfloat16)
    everyone = lax.all_gather(normed, both, axis=0, tiled=True)
    ex_local = w_gate.shape[0]
    capacity = n_dp * GROUP_CAP
    own = column * ex_local + jnp.arange(ex_local, dtype=jnp.int32)
    is_first = all_routes[None, :, 0] == own[:, None]
    is_second = all_routes[None, :, 1] == own[:, None]
    member = is_first | is_second
    index = jnp.arange(tokens)
    earlier = (index[:, None] < index[None, :]).astype(jnp.bfloat16)
    place = jnp.dot(
        member.astype(jnp.bfloat16), earlier, preferred_element_type=jnp.float32
    ).astype(jnp.int32)
    picker = member[:, None, :] & (place[:, None, :] == jnp.arange(capacity)[None, :, None])
    compact = jnp.dot(
        picker.astype(jnp.bfloat16).reshape(ex_local * capacity, tokens),
        everyone,
        preferred_element_type=jnp.float32,
    ).astype(jnp.bfloat16)
    compact = compact.reshape(ex_local, capacity, width)
    logits = jnp.dot(everyone, router, preferred_element_type=jnp.float32)
    ids = jnp.arange(EXPERTS, dtype=jnp.int32)
    first_logit = jnp.sum(jnp.where(all_routes[:, 0:1] == ids, logits, 0.0), axis=-1)
    second_logit = jnp.sum(jnp.where(all_routes[:, 1:2] == ids, logits, 0.0), axis=-1)
    gates = jnp.where(
        is_first,
        jax.nn.sigmoid(first_logit - second_logit)[None],
        jnp.where(is_second, jax.nn.sigmoid(second_logit - first_logit)[None], 0.0),
    )
    slot_gate = jnp.sum(jnp.where(picker, gates[:, None, :], 0.0), axis=-1)
    slot_span = jnp.sum(jnp.where(picker, index // WIN, 0), axis=-1)
    pool = jnp.where(
        slot_span[:, None, :] == jnp.arange(spans)[None, :, None], slot_gate[:, None, :], 0.0
    )
    gate_proj = jnp.einsum("end,edf->enf", compact, w_gate, preferred_element_type=jnp.float32)
    up_proj = jnp.einsum("end,edf->enf", compact, w_up, preferred_element_type=jnp.float32)
    hidden = (jax.nn.silu(gate_proj) * up_proj).astype(jnp.bfloat16)
    weighed = jnp.einsum("esn,enf->sef", pool, hidden.astype(jnp.float32), precision=exact)
    weighed = weighed.reshape(spans, -1)
    high = lax.reduce_precision(weighed, 8, 7)
    halves = jnp.concatenate([high, weighed - high], axis=0).astype(jnp.bfloat16)
    down = jnp.dot(halves, w_down.reshape(-1, width), preferred_element_type=jnp.float32)
    token_span = ((dp_index * n_ex + column) * tok_local + jnp.arange(tok_local)) // WIN
    pool_matrix = (token_span[None, :] == jnp.arange(spans)[:, None]).astype(jnp.float32)
    pooled = down[:spans] + down[spans:] + jnp.dot(pool_matrix, mixed, precision=exact)
    pooled = lax.all_to_all(
        pooled.reshape(spans, n_ex, -1).transpose(1, 0, 2),
        "expert",
        split_axis=0,
        concat_axis=0,
        tiled=True,
    )
    pooled = lax.psum(jnp.sum(pooled, axis=0), "dp")
    squares = lax.psum(jnp.sum(pooled * pooled, axis=-1), "expert")
    summary = (pooled * lax.rsqrt(squares / width + EPSILON)[:, None] * summary_gain).astype(
        jnp.bfloat16
    )
    heads_local = summary.shape[1] // HD
    others = summary.reshape(spans, heads_local, HD)
    summary = lax.dynamic_slice_in_dim(summary, dp_index * span_local, span_local)
    mine = summary.reshape(span_local, heads_local, HD)
    factor = reduce_scale / math.sqrt(HD)
    scores = (
        jnp.einsum("chd,khd->hck", mine, others, preferred_element_type=jnp.float32)
        * factor[:, None, None]
    )
    own_assign = lax.dynamic_slice_in_dim(assign, dp_index * span_local, span_local)
    same = own_assign[:, None] == assign[None, :]
    scores = jnp.where(same[None], scores, -jnp.inf)
    highest = jnp.max(scores, axis=-1, keepdims=True)
    expo = jnp.exp(scores - highest)
    weights = (expo / jnp.sum(expo, axis=-1, keepdims=True)).astype(jnp.bfloat16)
    reduced = jnp.einsum("hck,khd->chd", weights, others, preferred_element_type=jnp.float32)
    reduced = reduced.reshape(span_local, heads_local * HD).astype(jnp.bfloat16)
    return (summary, reduced)


def solution(mesh):
    return jax.shard_map(
        shards,
        mesh=mesh,
        in_specs=(
            P(("dp", "expert"), None),
            P("dp", "expert"),
            P("dp", "expert"),
            P("dp", "expert"),
            P("dp", None, "expert"),
            P("dp", None, "expert"),
            P("expert", "dp"),
            P(),
            P(),
            P(("dp", "expert"), None),
            P("expert", None, "dp"),
            P("expert", None, "dp"),
            P("expert", "dp", None),
            P("expert"),
            P("expert"),
            P(),
        ),
        out_specs=(P("dp", "expert"), P("dp", "expert")),
        check_vma=False,
    )
```

```python
import math

import jax
import jax.numpy as jnp
from jax import lax
from jax.sharding import PartitionSpec as P

HEADS = 32
KVH = 8
HD = 128
EXPERTS = 8
WIN = 32
GROUP_CAP = 24


EPSILON = 1e-05


def attend(queries, new_keys, new_values, cache_keys, cache_values):
    span_count, cache_len, kv_width = cache_keys.shape
    kv_local = kv_width // HD
    group = HEADS // KVH
    window = queries.shape[0] // span_count
    query_view = queries.reshape(span_count, window, kv_local, group, HD)
    fresh_keys = new_keys.reshape(span_count, window, kv_local, HD)
    fresh_values = new_values.reshape(span_count, window, kv_local, HD)
    stored_keys = cache_keys.reshape(span_count, cache_len, kv_local, HD)
    stored_values = cache_values.reshape(span_count, cache_len, kv_local, HD)
    factor = 1.0 / math.sqrt(HD)
    past_scores = (
        jnp.einsum("ctkgd,cpkd->ckgtp", query_view, stored_keys, preferred_element_type=jnp.float32)
        * factor
    )
    fresh_scores = (
        jnp.einsum("ctkgd,cskd->ckgts", query_view, fresh_keys, preferred_element_type=jnp.float32)
        * factor
    )
    causal = jnp.arange(window)[:, None] >= jnp.arange(window)[None, :]
    fresh_scores = jnp.where(causal, fresh_scores, -jnp.inf)
    highest = jnp.maximum(jnp.max(past_scores, axis=-1), jnp.max(fresh_scores, axis=-1))[..., None]
    past_exp = jnp.exp(past_scores - highest)
    fresh_exp = jnp.exp(fresh_scores - highest)
    totals = jnp.sum(past_exp, axis=-1, keepdims=True) + jnp.sum(fresh_exp, axis=-1, keepdims=True)
    past_weights = (past_exp / totals).astype(jnp.bfloat16)
    fresh_weights = (fresh_exp / totals).astype(jnp.bfloat16)
    context = jnp.einsum(
        "ckgtp,cpkd->ctkgd", past_weights, stored_values, preferred_element_type=jnp.float32
    )
    context = context + jnp.einsum(
        "ckgts,cskd->ctkgd", fresh_weights, fresh_values, preferred_element_type=jnp.float32
    )
    return context.astype(jnp.bfloat16).reshape(span_count * window, kv_local * group * HD)


def spread(block, axes):
    copies = jnp.broadcast_to(block[None], (lax.axis_size(axes), *block.shape))
    return lax.all_to_all(copies, axes, split_axis=0, concat_axis=0, tiled=True)


def shards(
    residual,
    queries,
    new_keys,
    new_values,
    cache_keys,
    cache_values,
    out_weight,
    ffn_gain,
    router,
    routes,
    w_gate,
    w_up,
    w_down,
    summary_gain,
    reduce_scale,
    assign,
):
    n_dp, n_ex = lax.axis_size("dp"), lax.axis_size("expert")
    dp_index, column = lax.axis_index("dp"), lax.axis_index("expert")
    both = ("dp", "expert")
    span_local = cache_keys.shape[0]
    tok_local, width = residual.shape
    tokens = tok_local * n_dp * n_ex
    spans = span_local * n_dp
    exact = lax.Precision.HIGHEST
    attended = attend(queries, new_keys, new_values, cache_keys, cache_values)
    rows = spread(attended, "dp").reshape(tokens, -1)
    parts = jnp.dot(rows, out_weight, preferred_element_type=jnp.float32).astype(jnp.bfloat16)
    labels = jnp.pad(routes.astype(jnp.bfloat16), ((0, 0), (0, HD - routes.shape[1])))
    labels = jnp.broadcast_to(labels[None], (n_dp * n_ex, *labels.shape))
    parts = jnp.concatenate([parts.reshape(n_dp * n_ex, tok_local, -1), labels], axis=-1)
    parts = lax.all_to_all(parts, both, split_axis=0, concat_axis=0, tiled=True)
    all_routes = parts[:, :, -HD : routes.shape[1] - HD].astype(jnp.int32).reshape(tokens, -1)
    parts = parts[:, :, :-HD]
    terms = jnp.sum(parts.reshape(n_dp, n_ex, tok_local, -1).astype(jnp.float32), axis=1)
    mixed = residual.astype(jnp.float32) + terms.transpose(1, 0, 2).reshape(tok_local, width)
    normed = (
        mixed * lax.rsqrt(jnp.mean(mixed * mixed, axis=-1, keepdims=True) + EPSILON) * ffn_gain
    ).astype(jnp.bfloat16)
    everyone = lax.all_gather(normed, both, axis=0, tiled=True)
    ex_local = w_gate.shape[0]
    capacity = n_dp * GROUP_CAP
    own = column * ex_local + jnp.arange(ex_local, dtype=jnp.int32)
    is_first = all_routes[None, :, 0] == own[:, None]
    is_second = all_routes[None, :, 1] == own[:, None]
    member = is_first | is_second
    index = jnp.arange(tokens)
    earlier = (index[:, None] < index[None, :]).astype(jnp.bfloat16)
    place = jnp.dot(
        member.astype(jnp.bfloat16), earlier, preferred_element_type=jnp.float32
    ).astype(jnp.int32)
    picker = member[:, None, :] & (place[:, None, :] == jnp.arange(capacity)[None, :, None])
    compact = jnp.dot(
        picker.astype(jnp.bfloat16).reshape(ex_local * capacity, tokens),
        everyone,
        preferred_element_type=jnp.float32,
    ).astype(jnp.bfloat16)
    compact = compact.reshape(ex_local, capacity, width)
    logits = jnp.dot(everyone, router, preferred_element_type=jnp.float32)
    ids = jnp.arange(EXPERTS, dtype=jnp.int32)
    first_logit = jnp.sum(jnp.where(all_routes[:, 0:1] == ids, logits, 0.0), axis=-1)
    second_logit = jnp.sum(jnp.where(all_routes[:, 1:2] == ids, logits, 0.0), axis=-1)
    gates = jnp.where(
        is_first,
        jax.nn.sigmoid(first_logit - second_logit)[None],
        jnp.where(is_second, jax.nn.sigmoid(second_logit - first_logit)[None], 0.0),
    )
    slot_gate = jnp.sum(jnp.where(picker, gates[:, None, :], 0.0), axis=-1)
    slot_span = jnp.sum(jnp.where(picker, index // WIN, 0), axis=-1)
    pool = jnp.where(
        slot_span[:, None, :] == jnp.arange(spans)[None, :, None], slot_gate[:, None, :], 0.0
    )
    gate_proj = jnp.einsum("end,edf->enf", compact, w_gate, preferred_element_type=jnp.float32)
    up_proj = jnp.einsum("end,edf->enf", compact, w_up, preferred_element_type=jnp.float32)
    hidden = (jax.nn.silu(gate_proj) * up_proj).astype(jnp.bfloat16)
    weighed = jnp.einsum("esn,enf->sef", pool, hidden.astype(jnp.float32), precision=exact)
    weighed = weighed.reshape(spans, -1)
    high = lax.reduce_precision(weighed, 8, 7)
    halves = jnp.concatenate([high, weighed - high], axis=0).astype(jnp.bfloat16)
    down = jnp.dot(halves, w_down.reshape(-1, width), preferred_element_type=jnp.float32)
    token_span = ((dp_index * n_ex + column) * tok_local + jnp.arange(tok_local)) // WIN
    pool_matrix = (token_span[None, :] == jnp.arange(spans)[:, None]).astype(jnp.float32)
    pooled = down[:spans] + down[spans:] + jnp.dot(pool_matrix, mixed, precision=exact)
    pooled = pooled.reshape(n_dp, span_local, n_ex, -1).transpose(0, 2, 1, 3)
    pooled = pooled.reshape(n_dp * n_ex, span_local, -1)
    pooled = lax.all_to_all(pooled, both, split_axis=0, concat_axis=0, tiled=True)
    pooled = jnp.sum(pooled, axis=0)
    pooled = spread(pooled, both).reshape(n_dp, n_ex, span_local, -1)
    pooled = pooled.transpose(0, 2, 1, 3).reshape(spans, n_ex, -1)
    squares = jnp.sum(pooled * pooled, axis=(1, 2))
    pooled = lax.dynamic_index_in_dim(pooled, column, axis=1, keepdims=False)
    summary = (pooled * lax.rsqrt(squares / width + EPSILON)[:, None] * summary_gain).astype(
        jnp.bfloat16
    )
    heads_local = summary.shape[1] // HD
    others = summary.reshape(spans, heads_local, HD)
    summary = lax.dynamic_slice_in_dim(summary, dp_index * span_local, span_local)
    mine = summary.reshape(span_local, heads_local, HD)
    factor = reduce_scale / math.sqrt(HD)
    scores = (
        jnp.einsum("chd,khd->hck", mine, others, preferred_element_type=jnp.float32)
        * factor[:, None, None]
    )
    own_assign = lax.dynamic_slice_in_dim(assign, dp_index * span_local, span_local)
    same = own_assign[:, None] == assign[None, :]
    scores = jnp.where(same[None], scores, -jnp.inf)
    highest = jnp.max(scores, axis=-1, keepdims=True)
    expo = jnp.exp(scores - highest)
    weights = (expo / jnp.sum(expo, axis=-1, keepdims=True)).astype(jnp.bfloat16)
    reduced = jnp.einsum("hck,khd->chd", weights, others, preferred_element_type=jnp.float32)
    reduced = reduced.reshape(span_local, heads_local * HD).astype(jnp.bfloat16)
    return (summary, reduced)


def solution(mesh):
    return jax.shard_map(
        shards,
        mesh=mesh,
        in_specs=(
            P(("dp", "expert"), None),
            P("dp", "expert"),
            P("dp", "expert"),
            P("dp", "expert"),
            P("dp", None, "expert"),
            P("dp", None, "expert"),
            P("expert", "dp"),
            P(),
            P(),
            P(("dp", "expert"), None),
            P("expert", None, "dp"),
            P("expert", None, "dp"),
            P("expert", "dp", None),
            P("expert"),
            P("expert"),
            P(),
        ),
        out_specs=(P("dp", "expert"), P("dp", "expert")),
        check_vma=False,
    )
```
